32 devices in a mesh: ingest: 8 (over y, x, core), section: 4 (over z).
Axes of the slice: x: 2, y: 2, z: 4, core: 2. Of those that a mesh axis runs over, the one named last changes fastest.
Arguments:
- txn_feats: bfloat16 [8192, 2048], P(('ingest', 'section')), may hold values from -6 to 6
- txn_seg: int32 [32, 256], P(('ingest', 'section')), may hold values from 0 to 63, as said below
- seg_row: int32 [32, 64], P(('ingest', 'section')), may hold values from 0 to 15, as said below
- send_counts: int32 [32, 8], P(('ingest', 'section')), may hold values from 0 to 8, as said below
- gains: float32 [4, 2048], P('section'), may hold values from 0.5 to 1.5
- tower_w: bfloat16 [4, 2048, 2048], P('section', 'ingest'), may hold values from -0.125 to 0.125
Outputs:
- card_embed: bfloat16 [512, 2048], P(('ingest', 'section'))
The draws below stay inside these ranges and needn't reach their ends.
Inputs may be any that keep to these rules, and one draw needn't show every extreme that they name: Each row of send_counts is at most 8 everywhere; in each section index one owner index gets exactly 8 from every device of that section; device 0 sends exactly 8 to every owner. Within a device's row txn_seg never falls, starts at 0 and ends at that device's sum of send_counts minus one. `seg_row`: the segments that one device sends to one owner name different card rows.
All inputs are finite; a program needn't handle non-finite values.
Results may differ from the reference program's by a relative error of at most 0.012.
Values may be sent and summed in bfloat16 or wider, within the bound.
A program may use at most 64 MiB of HBM per device.

```python
import jax
import jax.numpy as jnp
from jax import lax

D = 2048
TXN_DEV = 256
CARD_DEV = 16
CAP = 8
TXN = 8192
LAYERS = 4
N_INGEST = 8
N_SECTION = 4


def make_lists(key):
    base = jax.random.fold_in(key, 7)
    key_counts, key_hot, key_seg, key_perm, key_fill = jax.random.split(base, 5)
    devs = N_INGEST * N_SECTION
    slots = N_INGEST * CAP
    counts = jax.random.randint(key_counts, (devs, N_INGEST), 0, CAP + 1).astype(jnp.int32)
    hot = jax.random.randint(key_hot, (N_SECTION,), 0, N_INGEST).astype(jnp.int32)
    hot_dev = hot[jnp.arange(devs) % N_SECTION]
    owners = jnp.arange(N_INGEST, dtype=jnp.int32)
    counts = jnp.where(owners[None, :] == hot_dev[:, None], CAP, counts).astype(jnp.int32)
    first_dev = (jnp.arange(devs, dtype=jnp.int32) == 0)[:, None]
    counts = jnp.where(first_dev, CAP, counts).astype(jnp.int32)
    ends = jnp.cumsum(counts, axis=1).astype(jnp.int32)
    starts = ends - counts
    used = ends[:, -1]
    raw = jax.random.randint(key_seg, (devs, TXN_DEV), 0, 1 << 20).astype(jnp.int32)
    segs = jnp.sort(raw % used[:, None], axis=1).astype(jnp.int32)
    segs = segs.at[:, 0].set(0)
    segs = segs.at[:, -1].set(used - 1).astype(jnp.int32)
    table = jnp.tile(jnp.arange(CARD_DEV, dtype=jnp.int32)[None, :], (devs * N_INGEST, 1))
    perm = jax.random.permutation(key_perm, table, axis=1, independent=True).reshape(devs, N_INGEST * CARD_DEV)
    g = jnp.arange(slots, dtype=jnp.int32)
    owner = jnp.sum((g[None, :, None] >= ends[:, None, :]).astype(jnp.int32), axis=2)
    owner = jnp.minimum(owner, N_INGEST - 1)
    rank = g[None, :] - jnp.take_along_axis(starts, owner, axis=1)
    rank = jnp.clip(rank, 0, CARD_DEV - 1)
    picked = jnp.take_along_axis(perm, owner * CARD_DEV + rank, axis=1)
    filler = jax.random.randint(key_fill, (devs, slots), 0, CARD_DEV).astype(jnp.int32)
    rows = jnp.where(g[None, :] < used[:, None], picked, filler).astype(jnp.int32)
    return (counts, segs, rows)


def draw_txn_seg(key, part):
    return make_lists(key)[1]


def draw_seg_row(key, part):
    return make_lists(key)[2]


def draw_send_counts(key, part):
    return make_lists(key)[0]


def block_levels(own_key, extent, cuts, low, top_value):
    factor_of, own = 1.0, jax.random.fold_in(own_key, 6)
    for dim, blocks in cuts:
        draws = jnp.exp(jax.random.uniform(jax.random.fold_in(own, dim), (blocks,), jnp.float32, low / len(cuts), top_value / len(cuts)))
        factor_of = factor_of * jnp.repeat(draws, extent[dim] // blocks).reshape([-1 if axis == dim else 1 for axis in range(len(extent))])
    return factor_of


def normal_values(key, extent, spread, most, pieces=(), held_as=jnp.bfloat16):
    drawn = jax.random.normal(key, extent, jnp.float32) * spread
    if len(pieces) > 0:
        drawn = block_levels(key, extent, pieces, -0.22, 0.18) * drawn
    return jnp.clip(drawn, min=-most, max=most).astype(held_as)


def setup_inputs(seed: int = 0) -> dict:
    key_of = jax.random.split(jax.random.key(seed), 7)
    return {
        "txn_feats": normal_values(key_of[0], (TXN, D), 1.0, 6.0, ((0, 32),)),
        "txn_seg": draw_txn_seg(jax.random.fold_in(key_of[6], 71), 0),
        "seg_row": draw_seg_row(jax.random.fold_in(key_of[6], 71), 0),
        "send_counts": draw_send_counts(jax.random.fold_in(key_of[6], 71), 0),
        "gains": jnp.clip(1.0 + 0.1 * jax.random.normal(key_of[4], (LAYERS, D), jnp.float32), 0.5, 1.5),
        "tower_w": normal_values(key_of[5], (LAYERS, D, D), D ** -0.5, 0.125, ((0, 4), (1, 8))),
    }


def tower_layer(x, gain, weight):
    u = x.astype(jnp.float32)
    mean_sq = lax.optimization_barrier(jnp.mean(u * u, axis=-1, keepdims=True))
    normed = (u * lax.rsqrt(mean_sq + 1e-05) * gain).astype(jnp.bfloat16)
    y = jnp.dot(normed.astype(jnp.float32), weight.astype(jnp.float32), precision=lax.Precision.HIGHEST)
    return (u + jax.nn.silu(y)).astype(jnp.bfloat16)

def reference(txn_feats, txn_seg, seg_row, send_counts, gains, tower_w):
    devs = N_INGEST * N_SECTION
    slots = N_INGEST * CAP
    feats = txn_feats.reshape(devs, TXN_DEV, D)
    slot_ids = jnp.arange(slots, dtype=jnp.int32)

    def pool(d, table):
        part = lax.dynamic_index_in_dim(feats, d, 0, keepdims=False).astype(jnp.float32)
        seg = lax.dynamic_index_in_dim(txn_seg, d, 0, keepdims=False)
        rows = lax.dynamic_index_in_dim(seg_row, d, 0, keepdims=False)
        counts = lax.dynamic_index_in_dim(send_counts, d, 0, keepdims=False)
        onehot = (slot_ids[:, None] == seg[None, :]).astype(jnp.float32)
        sums = jnp.dot(onehot, part, precision=lax.Precision.HIGHEST).astype(jnp.bfloat16)
        sums = lax.optimization_barrier(sums).astype(jnp.float32)
        ends = jnp.cumsum(counts).astype(jnp.int32)
        owner = lax.optimization_barrier(jnp.sum((slot_ids[:, None] >= ends[None, :]).astype(jnp.int32), axis=1))
        valid = slot_ids < ends[-1]
        owner = jnp.minimum(owner, N_INGEST - 1)
        section_idx = (d % N_SECTION).astype(jnp.int32)
        target = ((owner * N_SECTION + section_idx) * CARD_DEV + rows).astype(jnp.int32)
        target = jnp.where(valid, target, 0).astype(jnp.int32)
        return table.at[target].add(sums * valid[:, None].astype(jnp.float32))
    table = lax.fori_loop(0, devs, pool, jnp.zeros((devs * CARD_DEV, D), jnp.float32))
    x = table.astype(jnp.bfloat16)
    for layer in range(N_SECTION):
        x = tower_layer(x, gains[layer], tower_w[layer])
    return x
```

```python
import functools

import jax
import jax.numpy as jnp
from jax import lax
from jax.experimental import pallas as pl
from jax.experimental.pallas import tpu as pltpu
from jax.sharding import PartitionSpec as P

MESH = pl.DeviceIdType.MESH
CARD_DEV = 16
LANES = 128

def from_behind(x, axis, by):
    count = lax.axis_size(axis)
    pairs = [(i, i + by) for i in range(count) if 0 <= i + by < count]
    return lax.ppermute(x, axis, pairs)


def broadcast(x, axis, root):
    mine = lax.axis_index(axis) == root
    return lax.psum(jnp.where(mine, x, jnp.zeros_like(x)), axis)


def tower_layer(x, gain, weight):
    u = x.astype(jnp.float32)
    mean_sq = jnp.mean(u * u, axis=-1, keepdims=True)
    normed = (u * lax.rsqrt(mean_sq + 1e-05) * gain).astype(jnp.bfloat16)
    y = jnp.dot(normed, weight, preferred_element_type=jnp.float32)
    return (u + jax.nn.silu(y)).astype(jnp.bfloat16)


def plain_body(txn_feats, txn_seg, seg_row, send_counts, gains, tower_w):
    width = txn_feats.shape[1]
    owners = lax.axis_size("ingest")
    sections = lax.axis_size("section")
    slots = seg_row.shape[1]
    cards = CARD_DEV
    weight = lax.all_gather(tower_w[0], "ingest", axis=0, tiled=True)
    gain = gains[0]
    counts = send_counts[0]
    ends = jnp.cumsum(counts)
    seg = txn_seg[0]
    rows = seg_row[0]
    slot_ids = jnp.arange(slots, dtype=jnp.int32)
    txn_owner = jnp.sum((seg[:, None] >= ends[None, :]).astype(jnp.int32), axis=1)
    txn_row = jnp.sum((seg[:, None] == slot_ids[None, :]).astype(jnp.int32) * rows[None, :], axis=1)
    target = txn_owner * cards + txn_row
    place = (jnp.arange(owners * cards, dtype=jnp.int32)[:, None] == target[None, :]).astype(
        jnp.bfloat16
    )
    buffer = jnp.dot(place, txn_feats, preferred_element_type=jnp.float32).astype(jnp.bfloat16)
    buffer = buffer.reshape(owners, cards, width)
    received = lax.all_to_all(buffer, "ingest", split_axis=0, concat_axis=0, tiled=True)
    pooled = jnp.sum(received, axis=0, dtype=jnp.float32).astype(jnp.bfloat16)
    section_pos = lax.axis_index("section")
    total_steps = 2 * sections - 1
    blocks = lax.all_gather(pooled[None], "section", axis=0, tiled=True)

    def advance(step, carry):
        current, finished, waiting = carry
        incoming = from_behind(current, "section", 1)
        fresh = lax.dynamic_index_in_dim(blocks, jnp.minimum(step, sections - 1), 0, keepdims=False)
        entry = jnp.where(section_pos == 0, fresh, incoming)
        active = (step >= section_pos) & (step < section_pos + sections)
        result = lax.cond(active, lambda v: tower_layer(v, gain, weight), lambda v: v, entry)
        place_at = jnp.clip(step - (sections - 1), 0, sections - 1)
        keep = (section_pos == sections - 1) & (step >= sections - 1)
        before = lax.dynamic_index_in_dim(finished, place_at, 0, keepdims=False)
        finished = lax.dynamic_update_index_in_dim(
            finished, jnp.where(keep, result, before), place_at, 0
        )
        return (result, finished, waiting)

    start_state = (
        jnp.zeros_like(pooled),
        jnp.zeros((sections, cards, width), jnp.bfloat16),
        pooled,
    )
    final_state = lax.fori_loop(0, total_steps, advance, start_state)
    everything = broadcast(final_state[1], "section", sections - 1)
    return lax.dynamic_index_in_dim(everything, section_pos, 0, keepdims=False)


def tower_kernel(
    owners, sections, cards,
    seg_ref, row_ref, count_ref, gain_ref, feats_hbm, w_hbm, out_ref,
    feats, w_all, parts, parts_in, pooled, xs, done, home,
    local_sem, w_send, w_recv, p_send, p_recv, x_send, z_send, z_recv, a_send, a_recv, r_send, r_recv,
):
    me = lax.axis_index("ingest")
    sec = lax.axis_index("section")
    devices = owners * sections
    flat = me * sections + sec
    width = feats.shape[1]
    fb = width // owners
    rows = owners * cards
    slots = row_ref.shape[1]
    core = lax.rem(me, 2)
    sibling = me + 1 - 2 * core
    chip = me // 2
    chips = owners // 2

    def remote(src, dst, send, recv, to):
        return pltpu.make_async_remote_copy(
            src_ref=src, dst_ref=dst, send_sem=send, recv_sem=recv, device_id=to, device_id_type=MESH
        )

    def cols(k):
        return pl.ds(pl.multiple_of(k * fb, LANES), fb)

    feats_copy = pltpu.make_async_copy(feats_hbm, feats, local_sem.at[0])
    feats_copy.start()
    w_copy = pltpu.make_async_copy(w_hbm.at[0, :, cols(me)], w_all.at[me], local_sem.at[1])
    w_copy.start()

    barrier = pltpu.get_barrier_semaphore()

    def greet(t, carry):
        other = lax.rem(flat + t, devices)
        pl.semaphore_signal(
            barrier, inc=1, device_id=(other // sections, lax.rem(other, sections)), device_id_type=MESH
        )
        return carry

    lax.fori_loop(1, devices, greet, 0)

    seg = seg_ref[...]
    owner = jnp.zeros_like(seg)
    end = count_ref[0, 0]
    for j in range(owners):
        if j > 0:
            end = end + count_ref[0, j]
        owner = owner + (seg >= end).astype(jnp.int32)
    row = jnp.zeros_like(seg)
    for g in range(slots):
        row = jnp.where(seg == g, row_ref[0, g], row)
    target = owner * cards + row
    ids = lax.broadcasted_iota(jnp.int32, (rows, seg.shape[1]), 0)
    place = jnp.where(ids == target, 1.0, 0.0).astype(jnp.bfloat16)
    feats_copy.wait()
    for k in range(owners):
        parts[k] = jnp.dot(
            place, feats[:, k * fb : (k + 1) * fb], preferred_element_type=jnp.float32
        ).astype(jnp.bfloat16)
    pl.semaphore_wait(barrier, devices - 1)

    def part_copy(t):
        to = lax.rem(me + t, owners)
        return remote(parts.at[to], parts_in.at[me], p_send.at[t], p_recv.at[me], (to, sec))

    def weight_copy(t):
        to = lax.rem(me + t, owners)
        return remote(w_hbm.at[0, :, cols(to)], w_all.at[me], w_send.at[t], w_recv.at[me], (to, sec))

    for t in range(1, owners):
        part_copy(t).start()
    for t in range(1, owners):
        weight_copy(t).start()

    total = parts[me].astype(jnp.float32)
    for t in range(1, owners):
        frm = lax.rem(me + owners - t, owners)
        remote(parts.at[me], parts_in.at[frm], p_send.at[t], p_recv.at[frm], (frm, sec)).wait_recv()
        total = total + parts_in[frm].astype(jnp.float32)
    pooled[...] = total.astype(jnp.bfloat16)

    def entry_copy():
        return remote(pooled, xs.at[sec, me], x_send.at[0], z_recv.at[sec], (me, 0))

    @pl.when(sec == 0)
    def _():
        xs[0, me] = pooled[...]

    @pl.when(sec > 0)
    def _():
        entry_copy().start()

    w_copy.wait()
    for t in range(1, owners):
        frm = lax.rem(me + owners - t, owners)
        remote(w_all.at[me], w_all.at[frm], w_send.at[t], w_recv.at[frm], (frm, sec)).wait_recv()

    def own_copy(m):
        block = xs.at[m, me]
        return remote(block, block, a_send.at[m, 0], a_recv.at[m, me], (sibling, sec))

    def cross_copy(m, d):
        block = xs.at[m, me]
        to = lax.rem(chip + d, chips) * 2 + core
        return remote(block, block, a_send.at[m, d], a_recv.at[m, me], (to, sec))

    def pass_copy(m, d):
        frm = lax.rem(chip + chips - d, chips) * 2 + core
        block = xs.at[m, frm]
        return remote(block, block, a_send.at[m, chips - 1 + d], a_recv.at[m, frm], (sibling, sec))

    def arrive(m, k):
        block = xs.at[m, k]
        remote(block, block, a_send.at[m, 0], a_recv.at[m, k], (sibling, sec)).wait_recv()

    def next_copy(m):
        return remote(done.at[m], xs.at[m, me], z_send.at[m], z_recv.at[m], (me, sec + 1))

    def home_copy(m, j):
        piece = done.at[m, pl.ds(j * cards, cards)]
        return remote(piece, home.at[me], r_send.at[m, j], r_recv.at[me], (j, m))

    last = sections - 1

    def each(m, carry):
        @pl.when(sec + m > 0)
        def _():
            block = xs.at[m, me]
            remote(block, block, z_send.at[m], z_recv.at[m], (me, 0)).wait_recv()

        for d in range(1, chips):
            cross_copy(m, d).start()
        own_copy(m).start()

        def term(k, acc, sq):
            u = xs[m, k].astype(jnp.float32)
            h = (u * gain_ref[:, cols(k)]).astype(jnp.bfloat16)
            acc = acc + jnp.dot(h, w_all[k], preferred_element_type=jnp.float32)
            return acc, sq + jnp.sum(u * u, axis=1, keepdims=True)

        acc = jnp.zeros((rows, fb), jnp.float32)
        sq = jnp.zeros((rows, 1), jnp.float32)
        acc, sq = term(me, acc, sq)
        arrive(m, sibling)
        acc, sq = term(sibling, acc, sq)
        for d in range(1, chips):
            k = lax.rem(chip + chips - d, chips) * 2 + core
            arrive(m, k)
            pass_copy(m, d).start()
            acc, sq = term(k, acc, sq)
        for d in range(1, chips):
            k = lax.rem(chip + chips - d, chips) * 2 + 1 - core
            arrive(m, k)
            acc, sq = term(k, acc, sq)
        y = acc * lax.rsqrt(sq / width + 1e-05)
        u = xs[m, me].astype(jnp.float32)
        done[m] = (u + y / (1.0 + jnp.exp(-y))).astype(jnp.bfloat16)

        @pl.when(sec < last)
        def _():
            next_copy(m).start()

        @pl.when(sec == last)
        def _():
            for j in range(owners):
                @pl.when((m < last) | (me != j))
                def _():
                    home_copy(m, j).start()

        return carry

    lax.fori_loop(0, sections, each, 0)

    for k in range(owners):
        @pl.when((sec != last) | (me != k))
        def _():
            remote(home.at[k], home.at[k], r_send.at[0, 0], r_recv.at[k], (k, last)).wait_recv()
            out_ref[:, k * fb : (k + 1) * fb] = home[k]

        @pl.when((sec == last) & (me == k))
        def _():
            out_ref[:, k * fb : (k + 1) * fb] = done[sections - 1, k * cards : (k + 1) * cards]

    for t in range(1, owners):
        part_copy(t).wait_send()
        weight_copy(t).wait_send()

    @pl.when(sec > 0)
    def _():
        entry_copy().wait_send()

    def finish(m, carry):
        own_copy(m).wait_send()
        for d in range(1, chips):
            cross_copy(m, d).wait_send()
            pass_copy(m, d).wait_send()

        @pl.when(sec < last)
        def _():
            next_copy(m).wait_send()

        @pl.when(sec == last)
        def _():
            for j in range(owners):
                @pl.when((m < last) | (me != j))
                def _():
                    home_copy(m, j).wait_send()

        return carry

    lax.fori_loop(0, sections, finish, 0)


def kernel_body(owners, sections, txn_feats, txn_seg, seg_row, send_counts, gains, tower_w):
    width = txn_feats.shape[1]
    fb = width // owners
    cards = CARD_DEV
    rows = owners * cards
    bf = jnp.bfloat16
    vmem = pl.BlockSpec(memory_space=pltpu.VMEM)
    smem = pl.BlockSpec(memory_space=pltpu.SMEM)
    anywhere = pl.BlockSpec(memory_space=pl.ANY)
    dma = pltpu.SemaphoreType.DMA
    return pl.pallas_call(
        functools.partial(tower_kernel, owners, sections, cards),
        out_shape=jax.ShapeDtypeStruct((cards, width), bf),
        in_specs=[vmem, smem, smem, vmem, anywhere, anywhere],
        out_specs=vmem,
        scratch_shapes=[
            pltpu.VMEM(txn_feats.shape, bf),
            pltpu.VMEM((owners, fb, fb), bf),
            pltpu.VMEM((owners, rows, fb), bf),
            pltpu.VMEM((owners, rows, fb), bf),
            pltpu.VMEM((rows, fb), bf),
            pltpu.VMEM((sections, owners, rows, fb), bf),
            pltpu.VMEM((sections, rows, fb), bf),
            pltpu.VMEM((owners, cards, fb), bf),
            dma((2,)),
            dma((owners,)),
            dma((owners,)),
            dma((owners,)),
            dma((owners,)),
            dma((1,)),
            dma((sections,)),
            dma((sections,)),
            dma((sections, owners)),
            dma((sections, owners)),
            dma((sections, owners)),
            dma((owners,)),
        ],
        compiler_params=pltpu.CompilerParams(
            collective_id=0, has_side_effects=True, vmem_limit_bytes=32 * 1024 * 1024
        ),
    )(txn_seg, seg_row, send_counts, gains, txn_feats, tower_w)


def solution(mesh):
    in_specs = (
        P(("ingest", "section"), None),
        P(("ingest", "section"), None),
        P(("ingest", "section"), None),
        P(("ingest", "section"), None),
        P("section", None),
        P("section", "ingest", None),
    )
    out_specs = P(("ingest", "section"), None)
    owners, sections = mesh.shape["ingest"], mesh.shape["section"]

    def body(txn_feats, txn_seg, seg_row, send_counts, gains, tower_w):
        args = (txn_feats, txn_seg, seg_row, send_counts, gains, tower_w)
        if owners % 2 == 0 and txn_feats.shape[1] % (owners * LANES) == 0:
            return kernel_body(owners, sections, *args)
        return plain_body(*args)

    return jax.shard_map(body, mesh=mesh, in_specs=in_specs, out_specs=out_specs, check_vma=False)
```

```python
import functools

import jax
import jax.numpy as jnp
from jax import lax
from jax.experimental import pallas as pl
from jax.experimental.pallas import tpu as pltpu
from jax.sharding import PartitionSpec as P

MESH = pl.DeviceIdType.MESH
CARD_DEV = 16
LANES = 128

def from_behind(x, axis, by):
    count = lax.axis_size(axis)
    pairs = [(i, i + by) for i in range(count) if 0 <= i + by < count]
    return lax.ppermute(x, axis, pairs)


def broadcast(x, axis, root):
    mine = lax.axis_index(axis) == root
    return lax.psum(jnp.where(mine, x, jnp.zeros_like(x)), axis)


def tower_layer(x, gain, weight):
    u = x.astype(jnp.float32)
    mean_sq = jnp.mean(u * u, axis=-1, keepdims=True)
    normed = (u * lax.rsqrt(mean_sq + 1e-05) * gain).astype(jnp.bfloat16)
    y = jnp.dot(normed, weight, preferred_element_type=jnp.float32)
    return (u + jax.nn.silu(y)).astype(jnp.bfloat16)


def plain_body(txn_feats, txn_seg, seg_row, send_counts, gains, tower_w):
    width = txn_feats.shape[1]
    owners = lax.axis_size("ingest")
    sections = lax.axis_size("section")
    slots = seg_row.shape[1]
    cards = CARD_DEV
    weight = lax.all_gather(tower_w[0], "ingest", axis=0, tiled=True)
    gain = gains[0]
    counts = send_counts[0]
    ends = jnp.cumsum(counts)
    seg = txn_seg[0]
    rows = seg_row[0]
    slot_ids = jnp.arange(slots, dtype=jnp.int32)
    txn_owner = jnp.sum((seg[:, None] >= ends[None, :]).astype(jnp.int32), axis=1)
    txn_row = jnp.sum((seg[:, None] == slot_ids[None, :]).astype(jnp.int32) * rows[None, :], axis=1)
    target = txn_owner * cards + txn_row
    place = (jnp.arange(owners * cards, dtype=jnp.int32)[:, None] == target[None, :]).astype(
        jnp.bfloat16
    )
    buffer = jnp.dot(place, txn_feats, preferred_element_type=jnp.float32).astype(jnp.bfloat16)
    buffer = buffer.reshape(owners, cards, width)
    received = lax.all_to_all(buffer, "ingest", split_axis=0, concat_axis=0, tiled=True)
    pooled = jnp.sum(received, axis=0, dtype=jnp.float32).astype(jnp.bfloat16)
    section_pos = lax.axis_index("section")
    total_steps = 2 * sections - 1
    blocks = lax.all_gather(pooled[None], "section", axis=0, tiled=True)

    def advance(step, carry):
        current, finished, waiting = carry
        incoming = from_behind(current, "section", 1)
        fresh = lax.dynamic_index_in_dim(blocks, jnp.minimum(step, sections - 1), 0, keepdims=False)
        entry = jnp.where(section_pos == 0, fresh, incoming)
        active = (step >= section_pos) & (step < section_pos + sections)
        result = lax.cond(active, lambda v: tower_layer(v, gain, weight), lambda v: v, entry)
        place_at = jnp.clip(step - (sections - 1), 0, sections - 1)
        keep = (section_pos == sections - 1) & (step >= sections - 1)
        before = lax.dynamic_index_in_dim(finished, place_at, 0, keepdims=False)
        finished = lax.dynamic_update_index_in_dim(
            finished, jnp.where(keep, result, before), place_at, 0
        )
        return (result, finished, waiting)

    start_state = (
        jnp.zeros_like(pooled),
        jnp.zeros((sections, cards, width), jnp.bfloat16),
        pooled,
    )
    final_state = lax.fori_loop(0, total_steps, advance, start_state)
    everything = broadcast(final_state[1], "section", sections - 1)
    return lax.dynamic_index_in_dim(everything, section_pos, 0, keepdims=False)


def tower_kernel(
    owners, sections, cards,
    seg_hbm, row_hbm, count_hbm, gain_hbm, feats_hbm, w_hbm, out_ref,
    seg_ref, row_ref, count_ref, gain_ref, feats, weight,
    sib_out, sib_in, own, cross_out, cross_in, sq_out, sq_in, pooled, xs, done, home,
    local_sem, sib_send, sib_recv, cross_send, cross_recv, sq_send, sq_recv,
    x_send, z_send, z_recv, r_send, r_recv,
):
    me = lax.axis_index("ingest")
    sec = lax.axis_index("section")
    last = sections - 1
    devices = owners * sections
    flat = me * sections + sec
    width = feats.shape[1]
    fb = width // owners
    rows = owners * cards
    slots = row_ref.shape[1]
    core = lax.rem(me, 2)
    sibling = me + 1 - 2 * core
    chip = me // 2
    chips = owners // 2

    def remote(src, dst, send, recv, to):
        return pltpu.make_async_remote_copy(
            src_ref=src, dst_ref=dst, send_sem=send, recv_sem=recv, device_id=to, device_id_type=MESH
        )

    def cols(k):
        return pl.ds(pl.multiple_of(k * fb, LANES), fb)

    loads = [
        pltpu.make_async_copy(source, to, local_sem.at[n])
        for n, (source, to) in enumerate((
            (seg_hbm, seg_ref), (row_hbm, row_ref), (count_hbm, count_ref),
            (feats_hbm, feats), (gain_hbm.at[:, cols(me)], gain_ref), (w_hbm.at[0], weight),
        ))
    ]
    for load in loads:
        load.start()

    barrier = pltpu.get_barrier_semaphore()

    def greet(t, carry):
        other = lax.rem(flat + t, devices)
        pl.semaphore_signal(
            barrier, inc=1, device_id=(other // sections, lax.rem(other, sections)), device_id_type=MESH
        )
        return carry

    lax.fori_loop(1, devices, greet, 0)
    for load in loads[:3]:
        load.wait()

    seg = seg_ref[...]
    owner = jnp.zeros_like(seg)
    end = count_ref[0, 0]
    for j in range(owners):
        if j > 0:
            end = end + count_ref[0, j]
        owner = owner + (seg >= end).astype(jnp.int32)
    row = jnp.zeros_like(seg)
    for g in range(slots):
        row = jnp.where(seg == g, row_ref[0, g], row)
    target = owner * cards + row
    ids = lax.broadcasted_iota(jnp.int32, (rows, seg.shape[1]), 0)
    place = jnp.where(ids == target, 1.0, 0.0).astype(jnp.bfloat16)
    loads[3].wait()
    pl.semaphore_wait(barrier, devices - 1)

    def ahead(d):
        return lax.rem(chip + d, chips)

    def behind(d):
        return lax.rem(chip + chips - d, chips)

    def sib_copy(q, d):
        c = ahead(d)
        return remote(sib_out.at[q, c], sib_in.at[q, c], sib_send.at[q, d], sib_recv.at[q, c], (sibling, sec))

    def cross_copy(q, d):
        return remote(
            cross_out.at[q, d], cross_in.at[q, chip], cross_send.at[q, d], cross_recv.at[q, chip],
            (ahead(d) * 2 + core, sec),
        )

    def cross_wait(q, d):
        c = behind(d)
        remote(
            cross_out.at[q, d], cross_in.at[q, c], cross_send.at[q, d], cross_recv.at[q, c], (c * 2 + core, sec)
        ).wait_recv()

    order = list(range(1, chips)) + [0]

    def reduced(q, product):
        for d in order:
            c = ahead(d)
            sib_out[q, c] = product(c * 2 + 1 - core).astype(jnp.bfloat16)
            sib_copy(q, d).start()
        for d in order:
            c = ahead(d)
            own[d] = product(c * 2 + core)
        for d in order[:-1]:
            sib_copy(q, d).wait_recv()
            cross_out[q, d] = (own[d] + sib_in[q, ahead(d)].astype(jnp.float32)).astype(jnp.bfloat16)
            cross_copy(q, d).start()
        sib_copy(q, 0).wait_recv()
        total = own[0] + sib_in[q, chip].astype(jnp.float32)
        for d in order[:-1]:
            cross_wait(q, d)
            total = total + cross_in[q, behind(d)].astype(jnp.float32)
        return total

    def reduced_sends(q):
        for d in order:
            sib_copy(q, d).wait_send()
        for d in order[:-1]:
            cross_copy(q, d).wait_send()

    x0 = reduced(
        sections, lambda k: jnp.dot(place, feats[:, cols(k)], preferred_element_type=jnp.float32)
    ).astype(jnp.bfloat16)

    def entry_copy():
        return remote(pooled, xs.at[sec], x_send.at[0], z_recv.at[sec], (me, 0))

    @pl.when(sec == 0)
    def _():
        xs[0] = x0

    @pl.when(sec > 0)
    def _():
        pooled[...] = x0
        entry_copy().start()

    loads[4].wait()
    loads[5].wait()

    def sq_copy(m, t):
        to = lax.rem(me + t, owners)
        return remote(sq_out.at[m], sq_in.at[m, me], sq_send.at[m, t], sq_recv.at[m, me], (to, sec))

    def sq_wait(m, t):
        frm = lax.rem(me + owners - t, owners)
        remote(sq_out.at[m], sq_in.at[m, frm], sq_send.at[m, t], sq_recv.at[m, frm], (frm, sec)).wait_recv()
        return sq_in[m, frm]

    def next_copy(m):
        return remote(done.at[m], xs.at[m], z_send.at[m], z_recv.at[m], (me, sec + 1))

    def home_copy(m, j):
        piece = done.at[m, pl.ds(j * cards, cards)]
        return remote(piece, home.at[me], r_send.at[m, j], r_recv.at[me], (j, m))

    def each(m, carry):
        @pl.when(sec + m > 0)
        def _():
            remote(xs.at[m], xs.at[m], z_send.at[m], z_recv.at[m], (me, 0)).wait_recv()

        u = xs[m].astype(jnp.float32)
        h = (u * gain_ref[...]).astype(jnp.bfloat16)
        sq = jnp.broadcast_to(jnp.sum(u * u, axis=1, keepdims=True), (rows, LANES))
        sq_out[m] = jnp.transpose(sq)[:8]
        for t in range(1, owners):
            sq_copy(m, t).start()
        y = reduced(m, lambda k: jnp.dot(h, weight[:, cols(k)], preferred_element_type=jnp.float32))
        sq = sq_out[m]
        for t in range(1, owners):
            sq = sq + sq_wait(m, t)
        scale = lax.rsqrt(sq / width + 1e-05)
        y = y * jnp.transpose(scale)[:, :1]
        u = xs[m].astype(jnp.float32)
        done[m] = (u + y / (1.0 + jnp.exp(-y))).astype(jnp.bfloat16)

        @pl.when(sec < last)
        def _():
            next_copy(m).start()

        @pl.when(sec == last)
        def _():
            for j in range(owners):
                @pl.when((m < last) | (me != j))
                def _():
                    home_copy(m, j).start()

        return carry

    lax.fori_loop(0, sections, each, 0)

    for k in range(owners):
        @pl.when((sec != last) | (me != k))
        def _():
            remote(home.at[k], home.at[k], r_send.at[0, 0], r_recv.at[k], (k, last)).wait_recv()
            out_ref[:, k * fb : (k + 1) * fb] = home[k]

        @pl.when((sec == last) & (me == k))
        def _():
            out_ref[:, k * fb : (k + 1) * fb] = done[last, k * cards : (k + 1) * cards]

    reduced_sends(sections)

    @pl.when(sec > 0)
    def _():
        entry_copy().wait_send()

    def finish(m, carry):
        reduced_sends(m)
        for t in range(1, owners):
            sq_copy(m, t).wait_send()

        @pl.when(sec < last)
        def _():
            next_copy(m).wait_send()

        @pl.when(sec == last)
        def _():
            for j in range(owners):
                @pl.when((m < last) | (me != j))
                def _():
                    home_copy(m, j).wait_send()

        return carry

    lax.fori_loop(0, sections, finish, 0)


def kernel_body(owners, sections, txn_feats, txn_seg, seg_row, send_counts, gains, tower_w):
    width = txn_feats.shape[1]
    fb = width // owners
    cards = CARD_DEV
    rows = owners * cards
    chips = owners // 2
    bf = jnp.bfloat16
    hbm = pl.BlockSpec(memory_space=pltpu.HBM)
    dma = pltpu.SemaphoreType.DMA
    stages = sections + 1
    return pl.pallas_call(
        functools.partial(tower_kernel, owners, sections, cards),
        out_shape=jax.ShapeDtypeStruct((cards, width), bf),
        in_specs=[hbm] * 6,
        out_specs=pl.BlockSpec(memory_space=pltpu.VMEM),
        scratch_shapes=[
            pltpu.VMEM(txn_seg.shape, jnp.int32),
            pltpu.SMEM(seg_row.shape, jnp.int32),
            pltpu.SMEM(send_counts.shape, jnp.int32),
            pltpu.VMEM((1, fb), jnp.float32),
            pltpu.VMEM(txn_feats.shape, bf),
            pltpu.VMEM((fb, width), bf),
            pltpu.VMEM((stages, chips, rows, fb), bf),
            pltpu.VMEM((stages, chips, rows, fb), bf),
            pltpu.VMEM((chips, rows, fb), jnp.float32),
            pltpu.VMEM((stages, chips, rows, fb), bf),
            pltpu.VMEM((stages, chips, rows, fb), bf),
            pltpu.VMEM((sections, 8, rows), jnp.float32),
            pltpu.VMEM((sections, owners, 8, rows), jnp.float32),
            pltpu.VMEM((rows, fb), bf),
            pltpu.VMEM((sections, rows, fb), bf),
            pltpu.VMEM((sections, rows, fb), bf),
            pltpu.VMEM((owners, cards, fb), bf),
            dma((6,)),
            dma((stages, chips)),
            dma((stages, chips)),
            dma((stages, chips)),
            dma((stages, chips)),
            dma((sections, owners)),
            dma((sections, owners)),
            dma((1,)),
            dma((sections,)),
            dma((sections,)),
            dma((sections, owners)),
            dma((owners,)),
        ],
        compiler_params=pltpu.CompilerParams(
            collective_id=0, has_side_effects=True, vmem_limit_bytes=64 * 1024 * 1024
        ),
    )(txn_seg, seg_row, send_counts, gains, txn_feats, tower_w)


def solution(mesh):
    in_specs = (
        P(("ingest", "section"), None),
        P(("ingest", "section"), None),
        P(("ingest", "section"), None),
        P(("ingest", "section"), None),
        P("section", None),
        P("section", "ingest", None),
    )
    out_specs = P(("ingest", "section"), None)
    owners, sections = mesh.shape["ingest"], mesh.shape["section"]

    def body(txn_feats, txn_seg, seg_row, send_counts, gains, tower_w):
        args = (txn_feats, txn_seg, seg_row, send_counts, gains, tower_w)
        if owners % 2 == 0 and owners * CARD_DEV % LANES == 0 and txn_feats.shape[1] % (owners * LANES) == 0:
            return kernel_body(owners, sections, *args)
        return plain_body(*args)

    return jax.shard_map(body, mesh=mesh, in_specs=in_specs, out_specs=out_specs, check_vma=False)
```

```python
import functools

import jax
import jax.numpy as jnp
from jax import lax
from jax.experimental import pallas as pl
from jax.experimental.pallas import tpu as pltpu
from jax.sharding import PartitionSpec as P

MESH = pl.DeviceIdType.MESH
CARD_DEV = 16
LANES = 128

def from_behind(x, axis, by):
    count = lax.axis_size(axis)
    pairs = [(i, i + by) for i in range(count) if 0 <= i + by < count]
    return lax.ppermute(x, axis, pairs)


def broadcast(x, axis, root):
    mine = lax.axis_index(axis) == root
    return lax.psum(jnp.where(mine, x, jnp.zeros_like(x)), axis)


def tower_layer(x, gain, weight):
    u = x.astype(jnp.float32)
    mean_sq = jnp.mean(u * u, axis=-1, keepdims=True)
    normed = (u * lax.rsqrt(mean_sq + 1e-05) * gain).astype(jnp.bfloat16)
    y = jnp.dot(normed, weight, preferred_element_type=jnp.float32)
    return (u + jax.nn.silu(y)).astype(jnp.bfloat16)


def plain_body(txn_feats, txn_seg, seg_row, send_counts, gains, tower_w):
    width = txn_feats.shape[1]
    owners = lax.axis_size("ingest")
    sections = lax.axis_size("section")
    slots = seg_row.shape[1]
    cards = CARD_DEV
    weight = lax.all_gather(tower_w[0], "ingest", axis=0, tiled=True)
    gain = gains[0]
    counts = send_counts[0]
    ends = jnp.cumsum(counts)
    seg = txn_seg[0]
    rows = seg_row[0]
    slot_ids = jnp.arange(slots, dtype=jnp.int32)
    txn_owner = jnp.sum((seg[:, None] >= ends[None, :]).astype(jnp.int32), axis=1)
    txn_row = jnp.sum((seg[:, None] == slot_ids[None, :]).astype(jnp.int32) * rows[None, :], axis=1)
    target = txn_owner * cards + txn_row
    place = (jnp.arange(owners * cards, dtype=jnp.int32)[:, None] == target[None, :]).astype(
        jnp.bfloat16
    )
    buffer = jnp.dot(place, txn_feats, preferred_element_type=jnp.float32).astype(jnp.bfloat16)
    buffer = buffer.reshape(owners, cards, width)
    received = lax.all_to_all(buffer, "ingest", split_axis=0, concat_axis=0, tiled=True)
    pooled = jnp.sum(received, axis=0, dtype=jnp.float32).astype(jnp.bfloat16)
    section_pos = lax.axis_index("section")
    total_steps = 2 * sections - 1
    blocks = lax.all_gather(pooled[None], "section", axis=0, tiled=True)

    def advance(step, carry):
        current, finished, waiting = carry
        incoming = from_behind(current, "section", 1)
        fresh = lax.dynamic_index_in_dim(blocks, jnp.minimum(step, sections - 1), 0, keepdims=False)
        entry = jnp.where(section_pos == 0, fresh, incoming)
        active = (step >= section_pos) & (step < section_pos + sections)
        result = lax.cond(active, lambda v: tower_layer(v, gain, weight), lambda v: v, entry)
        place_at = jnp.clip(step - (sections - 1), 0, sections - 1)
        keep = (section_pos == sections - 1) & (step >= sections - 1)
        before = lax.dynamic_index_in_dim(finished, place_at, 0, keepdims=False)
        finished = lax.dynamic_update_index_in_dim(
            finished, jnp.where(keep, result, before), place_at, 0
        )
        return (result, finished, waiting)

    start_state = (
        jnp.zeros_like(pooled),
        jnp.zeros((sections, cards, width), jnp.bfloat16),
        pooled,
    )
    final_state = lax.fori_loop(0, total_steps, advance, start_state)
    everything = broadcast(final_state[1], "section", sections - 1)
    return lax.dynamic_index_in_dim(everything, section_pos, 0, keepdims=False)


def tower_kernel(
    owners, sections, cards,
    seg_hbm, row_hbm, count_hbm, gain_hbm, feats_hbm, w_hbm, out_ref,
    seg_ref, row_ref, count_ref, gain_ref, feats, weight,
    sib_out, sib_in, own, cross_out, cross_in, sq_out, sq_in, pooled, xs, done, back, home,
    local_sem, sib_send, sib_recv, cross_send, cross_recv, sq_send, sq_recv,
    x_send, z_send, z_recv, b_send, b_recv, r_send, r_recv,
):
    me = lax.axis_index("ingest")
    sec = lax.axis_index("section")
    last = sections - 1
    width = feats.shape[1]
    fb = width // owners
    rows = owners * cards
    slots = row_ref.shape[1]
    core = lax.rem(me, 2)
    sibling = me + 1 - 2 * core
    chip = me // 2
    chips = owners // 2

    def remote(src, dst, send, recv, to):
        return pltpu.make_async_remote_copy(
            src_ref=src, dst_ref=dst, send_sem=send, recv_sem=recv, device_id=to, device_id_type=MESH
        )

    def cols(k):
        return pl.ds(pl.multiple_of(k * fb, LANES), fb)

    loads = [
        pltpu.make_async_copy(source, to, local_sem.at[n])
        for n, (source, to) in enumerate((
            (seg_hbm, seg_ref), (row_hbm, row_ref), (count_hbm, count_ref),
            (feats_hbm, feats), (gain_hbm.at[:, cols(me)], gain_ref), (w_hbm.at[0], weight),
        ))
    ]
    for load in loads:
        load.start()

    barrier = pltpu.get_barrier_semaphore()

    for t in range(1, owners):
        pl.semaphore_signal(
            barrier, inc=1, device_id=(lax.rem(me + t, owners), sec), device_id_type=MESH
        )
    for t in range(1, sections):
        pl.semaphore_signal(
            barrier, inc=1, device_id=(me, lax.rem(sec + t, sections)), device_id_type=MESH
        )
    for load in loads[:3]:
        load.wait()

    seg = seg_ref[...]
    owner = jnp.zeros_like(seg)
    end = count_ref[0, 0]
    for j in range(owners):
        if j > 0:
            end = end + count_ref[0, j]
        owner = owner + (seg >= end).astype(jnp.int32)
    row = jnp.zeros_like(seg)
    for g in range(slots):
        row = jnp.where(seg == g, row_ref[0, g], row)
    target = owner * cards + row
    ids = lax.broadcasted_iota(jnp.int32, (rows, seg.shape[1]), 0)
    place = jnp.where(ids == target, 1.0, 0.0).astype(jnp.bfloat16)
    loads[3].wait()
    pl.semaphore_wait(barrier, owners + sections - 2)

    def ahead(d):
        return lax.rem(chip + d, chips)

    def behind(d):
        return lax.rem(chip + chips - d, chips)

    def sib_copy(q, d):
        c = ahead(d)
        return remote(sib_out.at[q, c], sib_in.at[q, c], sib_send.at[q, d], sib_recv.at[q, c], (sibling, sec))

    def cross_copy(q, d):
        return remote(
            cross_out.at[q, d], cross_in.at[q, chip], cross_send.at[q, d], cross_recv.at[q, chip],
            (ahead(d) * 2 + core, sec),
        )

    def cross_wait(q, d):
        c = behind(d)
        remote(
            cross_out.at[q, d], cross_in.at[q, c], cross_send.at[q, d], cross_recv.at[q, c], (c * 2 + core, sec)
        ).wait_recv()

    order = list(range(1, chips)) + [0]

    def reduced(q, product):
        for d in order:
            c = ahead(d)
            sib_out[q, c] = product(c * 2 + 1 - core).astype(jnp.bfloat16)
            sib_copy(q, d).start()
        for d in order:
            c = ahead(d)
            own[d] = product(c * 2 + core)
        for d in order[:-1]:
            sib_copy(q, d).wait_recv()
            cross_out[q, d] = (own[d] + sib_in[q, ahead(d)].astype(jnp.float32)).astype(jnp.bfloat16)
            cross_copy(q, d).start()
        sib_copy(q, 0).wait_recv()
        total = own[0] + sib_in[q, chip].astype(jnp.float32)
        for d in order[:-1]:
            cross_wait(q, d)
            total = total + cross_in[q, behind(d)].astype(jnp.float32)
        return total

    def reduced_sends(q):
        for d in order:
            sib_copy(q, d).wait_send()
        for d in order[:-1]:
            cross_copy(q, d).wait_send()

    x0 = reduced(
        sections, lambda k: jnp.dot(place, feats[:, cols(k)], preferred_element_type=jnp.float32)
    ).astype(jnp.bfloat16)

    def entry_copy():
        return remote(pooled, xs.at[sec], x_send.at[0], z_recv.at[sec], (me, 0))

    @pl.when(sec == 0)
    def _():
        xs[0] = x0

    @pl.when(sec > 0)
    def _():
        pooled[...] = x0
        entry_copy().start()

    loads[4].wait()
    loads[5].wait()

    def sq_copy(m, t):
        to = lax.rem(me + t, owners)
        return remote(sq_out.at[m], sq_in.at[m, me], sq_send.at[m, t], sq_recv.at[m, me], (to, sec))

    def sq_wait(m, t):
        frm = lax.rem(me + owners - t, owners)
        remote(sq_out.at[m], sq_in.at[m, frm], sq_send.at[m, t], sq_recv.at[m, frm], (frm, sec)).wait_recv()
        return sq_in[m, frm]

    def next_copy(m):
        return remote(done.at[m], xs.at[m], z_send.at[m], z_recv.at[m], (me, sec + 1))

    def back_copy(m):
        return remote(done.at[m], back, b_send.at[m], b_recv.at[0], (me, m))

    def home_copy(t):
        to = lax.rem(me + t, owners)
        piece = back.at[pl.ds(to * cards, cards)]
        return remote(piece, home.at[me], r_send.at[t], r_recv.at[me], (to, sec))

    def each(m, carry):
        @pl.when(sec + m > 0)
        def _():
            remote(xs.at[m], xs.at[m], z_send.at[m], z_recv.at[m], (me, 0)).wait_recv()

        u = xs[m].astype(jnp.float32)
        h = (u * gain_ref[...]).astype(jnp.bfloat16)
        sq = jnp.broadcast_to(jnp.sum(u * u, axis=1, keepdims=True), (rows, LANES))
        sq_out[m] = jnp.transpose(sq)[:8]
        for t in range(1, owners):
            sq_copy(m, t).start()
        y = reduced(m, lambda k: jnp.dot(h, weight[:, cols(k)], preferred_element_type=jnp.float32))
        sq = sq_out[m]
        for t in range(1, owners):
            sq = sq + sq_wait(m, t)
        scale = lax.rsqrt(sq / width + 1e-05)
        y = y * jnp.transpose(scale)[:, :1]
        u = xs[m].astype(jnp.float32)
        done[m] = (u + y / (1.0 + jnp.exp(-y))).astype(jnp.bfloat16)

        @pl.when(sec < last)
        def _():
            next_copy(m).start()

        @pl.when((sec == last) & (m < last))
        def _():
            back_copy(m).start()

        return carry

    lax.fori_loop(0, sections, each, 0)

    @pl.when(sec == last)
    def _():
        back[...] = done[last]

    @pl.when(sec < last)
    def _():
        remote(back, back, b_send.at[0], b_recv.at[0], (me, last)).wait_recv()

    for t in range(1, owners):
        home_copy(t).start()
    out_ref[:, cols(me)] = back[pl.ds(me * cards, cards)]
    for t in range(1, owners):
        frm = lax.rem(me + owners - t, owners)
        remote(home.at[frm], home.at[frm], r_send.at[t], r_recv.at[frm], (frm, sec)).wait_recv()
        out_ref[:, cols(frm)] = home[frm]
        home_copy(t).wait_send()

    reduced_sends(sections)

    @pl.when(sec > 0)
    def _():
        entry_copy().wait_send()

    def finish(m, carry):
        reduced_sends(m)
        for t in range(1, owners):
            sq_copy(m, t).wait_send()

        @pl.when(sec < last)
        def _():
            next_copy(m).wait_send()

        @pl.when((sec == last) & (m < last))
        def _():
            back_copy(m).wait_send()

        return carry

    lax.fori_loop(0, sections, finish, 0)


def kernel_body(owners, sections, txn_feats, txn_seg, seg_row, send_counts, gains, tower_w):
    width = txn_feats.shape[1]
    fb = width // owners
    cards = CARD_DEV
    rows = owners * cards
    chips = owners // 2
    bf = jnp.bfloat16
    hbm = pl.BlockSpec(memory_space=pltpu.HBM)
    dma = pltpu.SemaphoreType.DMA
    stages = sections + 1
    return pl.pallas_call(
        functools.partial(tower_kernel, owners, sections, cards),
        out_shape=jax.ShapeDtypeStruct((cards, width), bf),
        in_specs=[hbm] * 6,
        out_specs=pl.BlockSpec(memory_space=pltpu.VMEM),
        scratch_shapes=[
            pltpu.VMEM(txn_seg.shape, jnp.int32),
            pltpu.SMEM(seg_row.shape, jnp.int32),
            pltpu.SMEM(send_counts.shape, jnp.int32),
            pltpu.VMEM((1, fb), jnp.float32),
            pltpu.VMEM(txn_feats.shape, bf),
            pltpu.VMEM((fb, width), bf),
            pltpu.VMEM((stages, chips, rows, fb), bf),
            pltpu.VMEM((stages, chips, rows, fb), bf),
            pltpu.VMEM((chips, rows, fb), jnp.float32),
            pltpu.VMEM((stages, chips, rows, fb), bf),
            pltpu.VMEM((stages, chips, rows, fb), bf),
            pltpu.VMEM((sections, 8, rows), jnp.float32),
            pltpu.VMEM((sections, owners, 8, rows), jnp.float32),
            pltpu.VMEM((rows, fb), bf),
            pltpu.VMEM((sections, rows, fb), bf),
            pltpu.VMEM((sections, rows, fb), bf),
            pltpu.VMEM((rows, fb), bf),
            pltpu.VMEM((owners, cards, fb), bf),
            dma((6,)),
            dma((stages, chips)),
            dma((stages, chips)),
            dma((stages, chips)),
            dma((stages, chips)),
            dma((sections, owners)),
            dma((sections, owners)),
            dma((1,)),
            dma((sections,)),
            dma((sections,)),
            dma((sections,)),
            dma((1,)),
            dma((owners,)),
            dma((owners,)),
        ],
        compiler_params=pltpu.CompilerParams(
            collective_id=0, has_side_effects=True, vmem_limit_bytes=64 * 1024 * 1024
        ),
    )(txn_seg, seg_row, send_counts, gains, txn_feats, tower_w)


def solution(mesh):
    in_specs = (
        P(("ingest", "section"), None),
        P(("ingest", "section"), None),
        P(("ingest", "section"), None),
        P(("ingest", "section"), None),
        P("section", None),
        P("section", "ingest", None),
    )
    out_specs = P(("ingest", "section"), None)
    owners, sections = mesh.shape["ingest"], mesh.shape["section"]

    def body(txn_feats, txn_seg, seg_row, send_counts, gains, tower_w):
        args = (txn_feats, txn_seg, seg_row, send_counts, gains, tower_w)
        if owners % 2 == 0 and owners * CARD_DEV % LANES == 0 and txn_feats.shape[1] % (owners * LANES) == 0:
            return kernel_body(owners, sections, *args)
        return plain_body(*args)

    return jax.shard_map(body, mesh=mesh, in_specs=in_specs, out_specs=out_specs, check_vma=False)
```

```python
import functools

import jax
import jax.numpy as jnp
from jax import lax
from jax.experimental import pallas as pl
from jax.experimental.pallas import tpu as pltpu
from jax.sharding import PartitionSpec as P

MESH = pl.DeviceIdType.MESH
CARD_DEV = 16
LANES = 128

def from_behind(x, axis, by):
    count = lax.axis_size(axis)
    pairs = [(i, i + by) for i in range(count) if 0 <= i + by < count]
    return lax.ppermute(x, axis, pairs)


def broadcast(x, axis, root):
    mine = lax.axis_index(axis) == root
    return lax.psum(jnp.where(mine, x, jnp.zeros_like(x)), axis)


def tower_layer(x, gain, weight):
    u = x.astype(jnp.float32)
    mean_sq = jnp.mean(u * u, axis=-1, keepdims=True)
    normed = (u * lax.rsqrt(mean_sq + 1e-05) * gain).astype(jnp.bfloat16)
    y = jnp.dot(normed, weight, preferred_element_type=jnp.float32)
    return (u + jax.nn.silu(y)).astype(jnp.bfloat16)


def plain_body(txn_feats, txn_seg, seg_row, send_counts, gains, tower_w):
    width = txn_feats.shape[1]
    owners = lax.axis_size("ingest")
    sections = lax.axis_size("section")
    slots = seg_row.shape[1]
    cards = CARD_DEV
    weight = lax.all_gather(tower_w[0], "ingest", axis=0, tiled=True)
    gain = gains[0]
    counts = send_counts[0]
    ends = jnp.cumsum(counts)
    seg = txn_seg[0]
    rows = seg_row[0]
    slot_ids = jnp.arange(slots, dtype=jnp.int32)
    txn_owner = jnp.sum((seg[:, None] >= ends[None, :]).astype(jnp.int32), axis=1)
    txn_row = jnp.sum((seg[:, None] == slot_ids[None, :]).astype(jnp.int32) * rows[None, :], axis=1)
    target = txn_owner * cards + txn_row
    place = (jnp.arange(owners * cards, dtype=jnp.int32)[:, None] == target[None, :]).astype(
        jnp.bfloat16
    )
    buffer = jnp.dot(place, txn_feats, preferred_element_type=jnp.float32).astype(jnp.bfloat16)
    buffer = buffer.reshape(owners, cards, width)
    received = lax.all_to_all(buffer, "ingest", split_axis=0, concat_axis=0, tiled=True)
    pooled = jnp.sum(received, axis=0, dtype=jnp.float32).astype(jnp.bfloat16)
    section_pos = lax.axis_index("section")
    total_steps = 2 * sections - 1
    blocks = lax.all_gather(pooled[None], "section", axis=0, tiled=True)

    def advance(step, carry):
        current, finished, waiting = carry
        incoming = from_behind(current, "section", 1)
        fresh = lax.dynamic_index_in_dim(blocks, jnp.minimum(step, sections - 1), 0, keepdims=False)
        entry = jnp.where(section_pos == 0, fresh, incoming)
        active = (step >= section_pos) & (step < section_pos + sections)
        result = lax.cond(active, lambda v: tower_layer(v, gain, weight), lambda v: v, entry)
        place_at = jnp.clip(step - (sections - 1), 0, sections - 1)
        keep = (section_pos == sections - 1) & (step >= sections - 1)
        before = lax.dynamic_index_in_dim(finished, place_at, 0, keepdims=False)
        finished = lax.dynamic_update_index_in_dim(
            finished, jnp.where(keep, result, before), place_at, 0
        )
        return (result, finished, waiting)

    start_state = (
        jnp.zeros_like(pooled),
        jnp.zeros((sections, cards, width), jnp.bfloat16),
        pooled,
    )
    final_state = lax.fori_loop(0, total_steps, advance, start_state)
    everything = broadcast(final_state[1], "section", sections - 1)
    return lax.dynamic_index_in_dim(everything, section_pos, 0, keepdims=False)


def tower_kernel(
    owners, sections, cards,
    seg_hbm, row_hbm, count_hbm, gain_hbm, feats_hbm, w_hbm, out_ref,
    seg_ref, row_ref, count_ref, gain_ref, lhs, rhs,
    sib_out, sib_in, total_ref, cross_out, cross_in, sq_out, sq_in, pooled, xs, done, back, home,
    local_sem, sib_send, sib_recv, cross_send, cross_recv, sq_send, sq_recv,
    x_send, z_send, z_recv, b_send, b_recv, r_send, r_recv,
):
    me = lax.axis_index("ingest")
    sec = lax.axis_index("section")
    last = sections - 1
    width = feats_hbm.shape[1]
    fb = width // owners
    rows = owners * cards
    slots = row_ref.shape[1]
    core = lax.rem(me, 2)
    sibling = me + 1 - 2 * core
    chip = me // 2
    chips = owners // 2

    def remote(src, dst, send, recv, to):
        return pltpu.make_async_remote_copy(
            src_ref=src, dst_ref=dst, send_sem=send, recv_sem=recv, device_id=to, device_id_type=MESH
        )

    def cols(k):
        return pl.ds(pl.multiple_of(k * fb, LANES), fb)

    loads = [
        pltpu.make_async_copy(source, to, local_sem.at[n])
        for n, (source, to) in enumerate((
            (seg_hbm, seg_ref), (row_hbm, row_ref), (count_hbm, count_ref),
            (feats_hbm, rhs.at[0]), (gain_hbm.at[:, cols(me)], gain_ref), (w_hbm.at[0], rhs.at[1]),
        ))
    ]
    for load in loads:
        load.start()

    barrier = pltpu.get_barrier_semaphore()

    def loop(lo, hi, act):
        def step(t, carry):
            act(t)
            return carry

        lax.fori_loop(lo, hi, step, 0)

    def greet(t):
        pl.semaphore_signal(barrier, inc=1, device_id=(lax.rem(me + t, owners), sec), device_id_type=MESH)

    def greet_column(t):
        pl.semaphore_signal(barrier, inc=1, device_id=(me, lax.rem(sec + t, sections)), device_id_type=MESH)

    loop(1, owners, greet)
    loop(1, sections, greet_column)
    for load in loads[:3]:
        load.wait()

    seg = seg_ref[...]
    owner = jnp.zeros_like(seg)
    end = count_ref[0, 0]
    for j in range(owners):
        if j > 0:
            end = end + count_ref[0, j]
        owner = owner + (seg >= end).astype(jnp.int32)

    def name_rows(n, row):
        for g in range(8):
            row = jnp.where(seg == n * 8 + g, row_ref[0, n * 8 + g], row)
        return row

    row = lax.fori_loop(0, slots // 8, name_rows, jnp.zeros_like(seg))
    target = owner * cards + row
    ids = lax.broadcasted_iota(jnp.int32, (rows, seg.shape[1]), 0)
    lhs[...] = jnp.where(ids == target, 1.0, 0.0).astype(jnp.bfloat16)
    for load in loads[3:]:
        load.wait()
    pl.semaphore_wait(barrier, owners + sections - 2)

    def ahead(d):
        return lax.rem(chip + d, chips)

    def behind(d):
        return lax.rem(chip + chips - d, chips)

    def sib_copy(q, d):
        c = ahead(d)
        return remote(sib_out.at[q, c], sib_in.at[q, c], sib_send.at[q, d], sib_recv.at[q, c], (sibling, sec))

    def cross_copy(q, d):
        return remote(
            cross_out.at[q, d], cross_in.at[q, chip], cross_send.at[q, d], cross_recv.at[q, chip],
            (ahead(d) * 2 + core, sec),
        )

    def cross_wait(q, d):
        c = behind(d)
        remote(
            cross_out.at[q, d], cross_in.at[q, c], cross_send.at[q, d], cross_recv.at[q, c], (c * 2 + core, sec)
        ).wait_recv()

    def product(q, k):
        return jnp.dot(
            lhs[...], rhs[jnp.minimum(q, 1), :, cols(k)], preferred_element_type=jnp.float32
        )

    def reduced(q):
        def send_sibling(t):
            d = lax.rem(t, chips)
            c = ahead(d)
            sib_out[q, c] = product(q, c * 2 + 1 - core).astype(jnp.bfloat16)
            sib_copy(q, d).start()

        def send_across(t):
            d = lax.rem(t, chips)
            c = ahead(d)
            mine = product(q, c * 2 + core)
            sib_copy(q, d).wait_recv()
            mine = mine + sib_in[q, c].astype(jnp.float32)

            @pl.when(d > 0)
            def _():
                cross_out[q, d] = mine.astype(jnp.bfloat16)
                cross_copy(q, d).start()

            @pl.when(d == 0)
            def _():
                total_ref[...] = mine

        def add(d):
            cross_wait(q, d)
            total_ref[...] += cross_in[q, behind(d)].astype(jnp.float32)

        loop(1, chips + 1, send_sibling)
        loop(1, chips + 1, send_across)
        loop(1, chips, add)

    def reduced_sends(q):
        loop(0, chips, lambda d: sib_copy(q, d).wait_send())
        loop(1, chips, lambda d: cross_copy(q, d).wait_send())

    def entry_copy():
        return remote(pooled, xs.at[sec], x_send.at[0], z_recv.at[sec], (me, 0))

    def sq_copy(m, t):
        to = lax.rem(me + t, owners)
        return remote(sq_out.at[m], sq_in.at[m, me], sq_send.at[m, t], sq_recv.at[m, me], (to, sec))

    def sq_wait(m, t):
        frm = lax.rem(me + owners - t, owners)
        remote(sq_out.at[m], sq_in.at[m, frm], sq_send.at[m, t], sq_recv.at[m, frm], (frm, sec)).wait_recv()

    def next_copy(m):
        return remote(done.at[m], xs.at[m], z_send.at[m], z_recv.at[m], (me, sec + 1))

    def back_copy(m):
        return remote(done.at[m], back, b_send.at[m], b_recv.at[0], (me, m))

    def home_copy(t):
        to = lax.rem(me + t, owners)
        piece = back.at[pl.ds(to * cards, cards)]
        return remote(piece, home.at[me], r_send.at[t], r_recv.at[me], (to, sec))

    def enter(m):
        @pl.when(sec + m > 0)
        def _():
            remote(xs.at[m], xs.at[m], z_send.at[m], z_recv.at[m], (me, 0)).wait_recv()

        u = xs[m].astype(jnp.float32)
        lhs[...] = (u * gain_ref[...]).astype(jnp.bfloat16)
        sq = jnp.broadcast_to(jnp.sum(u * u, axis=1, keepdims=True), (rows, LANES))
        sq_out[m] = jnp.transpose(sq)[:8]
        loop(1, owners, lambda t: sq_copy(m, t).start())

    def leave(m):
        def add_sq(t, sq):
            sq_wait(m, t)
            return sq + sq_in[m, lax.rem(me + owners - t, owners)]

        sq = lax.fori_loop(1, owners, add_sq, sq_out[m])
        scale = lax.rsqrt(sq / width + 1e-05)
        y = total_ref[...] * jnp.transpose(scale)[:, :1]
        u = xs[m].astype(jnp.float32)
        done[m] = (u + y / (1.0 + jnp.exp(-y))).astype(jnp.bfloat16)

        @pl.when(sec < last)
        def _():
            next_copy(m).start()

        @pl.when((sec == last) & (m < last))
        def _():
            back_copy(m).start()

    def leave_pool():
        @pl.when(sec == 0)
        def _():
            xs[0] = total_ref[...].astype(jnp.bfloat16)

        @pl.when(sec > 0)
        def _():
            pooled[...] = total_ref[...].astype(jnp.bfloat16)
            entry_copy().start()

    def each(q):
        @pl.when(q > 0)
        def _():
            enter(q - 1)

        reduced(q)

        @pl.when(q > 0)
        def _():
            leave(q - 1)

        @pl.when(q == 0)
        def _():
            leave_pool()

    loop(0, sections + 1, each)

    @pl.when(sec == last)
    def _():
        back[...] = done[last]

    @pl.when(sec < last)
    def _():
        remote(back, back, b_send.at[0], b_recv.at[0], (me, last)).wait_recv()

    loop(1, owners, lambda t: home_copy(t).start())
    out_ref[:, cols(me)] = back[pl.ds(me * cards, cards)]

    def gather(t):
        frm = lax.rem(me + owners - t, owners)
        remote(home.at[frm], home.at[frm], r_send.at[t], r_recv.at[frm], (frm, sec)).wait_recv()
        out_ref[:, cols(frm)] = home[frm]

    loop(1, owners, gather)
    loop(1, owners, lambda t: home_copy(t).wait_send())
    loop(0, sections + 1, reduced_sends)

    @pl.when(sec > 0)
    def _():
        entry_copy().wait_send()

    def finish(m):
        loop(1, owners, lambda t: sq_copy(m, t).wait_send())

        @pl.when(sec < last)
        def _():
            next_copy(m).wait_send()

        @pl.when((sec == last) & (m < last))
        def _():
            back_copy(m).wait_send()

    loop(0, sections, finish)


def kernel_body(owners, sections, txn_feats, txn_seg, seg_row, send_counts, gains, tower_w):
    width = txn_feats.shape[1]
    fb = width // owners
    cards = CARD_DEV
    rows = owners * cards
    chips = owners // 2
    bf = jnp.bfloat16
    hbm = pl.BlockSpec(memory_space=pltpu.HBM)
    dma = pltpu.SemaphoreType.DMA
    stages = sections + 1
    return pl.pallas_call(
        functools.partial(tower_kernel, owners, sections, cards),
        out_shape=jax.ShapeDtypeStruct((cards, width), bf),
        in_specs=[hbm] * 6,
        out_specs=pl.BlockSpec(memory_space=pltpu.VMEM),
        scratch_shapes=[
            pltpu.VMEM(txn_seg.shape, jnp.int32),
            pltpu.SMEM(seg_row.shape, jnp.int32),
            pltpu.SMEM(send_counts.shape, jnp.int32),
            pltpu.VMEM((1, fb), jnp.float32),
            pltpu.VMEM((rows, fb), bf),
            pltpu.VMEM((2, fb, width), bf),
            pltpu.VMEM((stages, chips, rows, fb), bf),
            pltpu.VMEM((stages, chips, rows, fb), bf),
            pltpu.VMEM((rows, fb), jnp.float32),
            pltpu.VMEM((stages, chips, rows, fb), bf),
            pltpu.VMEM((stages, chips, rows, fb), bf),
            pltpu.VMEM((sections, 8, rows), jnp.float32),
            pltpu.VMEM((sections, owners, 8, rows), jnp.float32),
            pltpu.VMEM((rows, fb), bf),
            pltpu.VMEM((sections, rows, fb), bf),
            pltpu.VMEM((sections, rows, fb), bf),
            pltpu.VMEM((rows, fb), bf),
            pltpu.VMEM((owners, cards, fb), bf),
            dma((6,)),
            dma((stages, chips)),
            dma((stages, chips)),
            dma((stages, chips)),
            dma((stages, chips)),
            dma((sections, owners)),
            dma((sections, owners)),
            dma((1,)),
            dma((sections,)),
            dma((sections,)),
            dma((sections,)),
            dma((1,)),
            dma((owners,)),
            dma((owners,)),
        ],
        compiler_params=pltpu.CompilerParams(
            collective_id=0, has_side_effects=True, vmem_limit_bytes=64 * 1024 * 1024
        ),
    )(txn_seg, seg_row, send_counts, gains, txn_feats, tower_w)


def solution(mesh):
    in_specs = (
        P(("ingest", "section"), None),
        P(("ingest", "section"), None),
        P(("ingest", "section"), None),
        P(("ingest", "section"), None),
        P("section", None),
        P("section", "ingest", None),
    )
    out_specs = P(("ingest", "section"), None)
    owners, sections = mesh.shape["ingest"], mesh.shape["section"]

    def body(txn_feats, txn_seg, seg_row, send_counts, gains, tower_w):
        args = (txn_feats, txn_seg, seg_row, send_counts, gains, tower_w)
        depth, width = txn_feats.shape
        whole = owners * CARD_DEV % LANES == 0 and width % (owners * LANES) == 0
        if owners % 2 == 0 and whole and depth == width // owners and seg_row.shape[1] % 8 == 0:
            return kernel_body(owners, sections, *args)
        return plain_body(*args)

    return jax.shard_map(body, mesh=mesh, in_specs=in_specs, out_specs=out_specs, check_vma=False)
```

```python
import functools

import jax
import jax.numpy as jnp
from jax import lax
from jax.experimental import pallas as pl
from jax.experimental.pallas import tpu as pltpu
from jax.sharding import PartitionSpec as P

MESH = pl.DeviceIdType.MESH
CARD_DEV = 16
LANES = 128

def from_behind(x, axis, by):
    count = lax.axis_size(axis)
    pairs = [(i, i + by) for i in range(count) if 0 <= i + by < count]
    return lax.ppermute(x, axis, pairs)


def broadcast(x, axis, root):
    mine = lax.axis_index(axis) == root
    return lax.psum(jnp.where(mine, x, jnp.zeros_like(x)), axis)


def tower_layer(x, gain, weight):
    u = x.astype(jnp.float32)
    mean_sq = jnp.mean(u * u, axis=-1, keepdims=True)
    normed = (u * lax.rsqrt(mean_sq + 1e-05) * gain).astype(jnp.bfloat16)
    y = jnp.dot(normed, weight, preferred_element_type=jnp.float32)
    return (u + jax.nn.silu(y)).astype(jnp.bfloat16)


def plain_body(txn_feats, txn_seg, seg_row, send_counts, gains, tower_w):
    width = txn_feats.shape[1]
    owners = lax.axis_size("ingest")
    sections = lax.axis_size("section")
    slots = seg_row.shape[1]
    cards = CARD_DEV
    weight = lax.all_gather(tower_w[0], "ingest", axis=0, tiled=True)
    gain = gains[0]
    counts = send_counts[0]
    ends = jnp.cumsum(counts)
    seg = txn_seg[0]
    rows = seg_row[0]
    slot_ids = jnp.arange(slots, dtype=jnp.int32)
    txn_owner = jnp.sum((seg[:, None] >= ends[None, :]).astype(jnp.int32), axis=1)
    txn_row = jnp.sum((seg[:, None] == slot_ids[None, :]).astype(jnp.int32) * rows[None, :], axis=1)
    target = txn_owner * cards + txn_row
    place = (jnp.arange(owners * cards, dtype=jnp.int32)[:, None] == target[None, :]).astype(
        jnp.bfloat16
    )
    buffer = jnp.dot(place, txn_feats, preferred_element_type=jnp.float32).astype(jnp.bfloat16)
    buffer = buffer.reshape(owners, cards, width)
    received = lax.all_to_all(buffer, "ingest", split_axis=0, concat_axis=0, tiled=True)
    pooled = jnp.sum(received, axis=0, dtype=jnp.float32).astype(jnp.bfloat16)
    section_pos = lax.axis_index("section")
    total_steps = 2 * sections - 1
    blocks = lax.all_gather(pooled[None], "section", axis=0, tiled=True)

    def advance(step, carry):
        current, finished, waiting = carry
        incoming = from_behind(current, "section", 1)
        fresh = lax.dynamic_index_in_dim(blocks, jnp.minimum(step, sections - 1), 0, keepdims=False)
        entry = jnp.where(section_pos == 0, fresh, incoming)
        active = (step >= section_pos) & (step < section_pos + sections)
        result = lax.cond(active, lambda v: tower_layer(v, gain, weight), lambda v: v, entry)
        place_at = jnp.clip(step - (sections - 1), 0, sections - 1)
        keep = (section_pos == sections - 1) & (step >= sections - 1)
        before = lax.dynamic_index_in_dim(finished, place_at, 0, keepdims=False)
        finished = lax.dynamic_update_index_in_dim(
            finished, jnp.where(keep, result, before), place_at, 0
        )
        return (result, finished, waiting)

    start_state = (
        jnp.zeros_like(pooled),
        jnp.zeros((sections, cards, width), jnp.bfloat16),
        pooled,
    )
    final_state = lax.fori_loop(0, total_steps, advance, start_state)
    everything = broadcast(final_state[1], "section", sections - 1)
    return lax.dynamic_index_in_dim(everything, section_pos, 0, keepdims=False)


def tower_kernel(
    owners, sections, cards,
    seg_hbm, row_hbm, count_hbm, gain_hbm, feats_hbm, w_hbm, out_ref,
    seg_ref, row_ref, count_ref, gain_ref, feats, weight,
    sib_out, sib_in, own, total_ref, cross_out, cross_in, sq_out, sq_in, pooled, xs, done, back, home,
    local_sem, sib_send, sib_recv, cross_send, cross_recv, sq_send, sq_recv,
    x_send, z_send, z_recv, b_send, b_recv, r_send, r_recv,
):
    me = lax.axis_index("ingest")
    sec = lax.axis_index("section")
    last = sections - 1
    width = feats.shape[1]
    fb = width // owners
    rows = owners * cards
    slots = row_ref.shape[1]
    core = lax.rem(me, 2)
    sibling = me + 1 - 2 * core
    chip = me // 2
    chips = owners // 2

    def remote(src, dst, send, recv, to):
        return pltpu.make_async_remote_copy(
            src_ref=src, dst_ref=dst, send_sem=send, recv_sem=recv, device_id=to, device_id_type=MESH
        )

    def cols(k):
        return pl.ds(pl.multiple_of(k * fb, LANES), fb)

    loads = [
        pltpu.make_async_copy(source, to, local_sem.at[n])
        for n, (source, to) in enumerate((
            (seg_hbm, seg_ref), (row_hbm, row_ref), (count_hbm, count_ref),
            (feats_hbm, feats), (gain_hbm.at[:, cols(me)], gain_ref), (w_hbm.at[0], weight),
        ))
    ]
    for load in loads:
        load.start()

    barrier = pltpu.get_barrier_semaphore()

    for t in range(1, owners):
        pl.semaphore_signal(
            barrier, inc=1, device_id=(lax.rem(me + t, owners), sec), device_id_type=MESH
        )
    for t in range(1, sections):
        pl.semaphore_signal(
            barrier, inc=1, device_id=(me, lax.rem(sec + t, sections)), device_id_type=MESH
        )
    for load in loads[:3]:
        load.wait()

    seg = seg_ref[...]
    owner = jnp.zeros_like(seg)
    end = count_ref[0, 0]
    for j in range(owners):
        if j > 0:
            end = end + count_ref[0, j]
        owner = owner + (seg >= end).astype(jnp.int32)
    row = jnp.zeros_like(seg)
    for g in range(slots):
        row = jnp.where(seg == g, row_ref[0, g], row)
    target = owner * cards + row
    ids = lax.broadcasted_iota(jnp.int32, (rows, seg.shape[1]), 0)
    place = jnp.where(ids == target, 1.0, 0.0).astype(jnp.bfloat16)
    loads[3].wait()
    pl.semaphore_wait(barrier, owners + sections - 2)

    def ahead(d):
        return lax.rem(chip + d, chips)

    def behind(d):
        return lax.rem(chip + chips - d, chips)

    def sib_copy(q, d):
        c = ahead(d)
        return remote(sib_out.at[q, c], sib_in.at[q, c], sib_send.at[q, d], sib_recv.at[q, c], (sibling, sec))

    def cross_copy(q, d):
        return remote(
            cross_out.at[q, d], cross_in.at[q, chip], cross_send.at[q, d], cross_recv.at[q, chip],
            (ahead(d) * 2 + core, sec),
        )

    def cross_wait(q, d):
        c = behind(d)
        remote(
            cross_out.at[q, d], cross_in.at[q, c], cross_send.at[q, d], cross_recv.at[q, c], (c * 2 + core, sec)
        ).wait_recv()

    order = list(range(1, chips)) + [0]

    def share(q, product):
        for d in order:
            c = ahead(d)
            sib_out[q, c] = product(c * 2 + 1 - core).astype(jnp.bfloat16)
            sib_copy(q, d).start()
        for d in order:
            own[d] = product(ahead(d) * 2 + core)

    def across(q):
        for d in order[:-1]:
            sib_copy(q, d).wait_recv()
            cross_out[q, d] = (own[d] + sib_in[q, ahead(d)].astype(jnp.float32)).astype(jnp.bfloat16)
            cross_copy(q, d).start()
        sib_copy(q, 0).wait_recv()
        total_ref[...] = own[0] + sib_in[q, chip].astype(jnp.float32)

    def collect(q):
        total = total_ref[...]
        for d in order[:-1]:
            cross_wait(q, d)
            total = total + cross_in[q, behind(d)].astype(jnp.float32)
        return total

    def reduced_sends(q):
        for d in order:
            sib_copy(q, d).wait_send()
        for d in order[:-1]:
            cross_copy(q, d).wait_send()

    share(sections, lambda k: jnp.dot(place, feats[:, cols(k)], preferred_element_type=jnp.float32))
    across(sections)
    x0 = collect(sections).astype(jnp.bfloat16)

    def entry_copy():
        return remote(pooled, xs.at[sec], x_send.at[0], z_recv.at[sec], (me, 0))

    @pl.when(sec == 0)
    def _():
        xs[0] = x0

    @pl.when(sec > 0)
    def _():
        pooled[...] = x0
        entry_copy().start()

    loads[4].wait()
    loads[5].wait()

    def sq_copy(m, t):
        to = lax.rem(me + t, owners)
        return remote(sq_out.at[m], sq_in.at[m, me], sq_send.at[m, t], sq_recv.at[m, me], (to, sec))

    def sq_wait(m, t):
        frm = lax.rem(me + owners - t, owners)
        remote(sq_out.at[m], sq_in.at[m, frm], sq_send.at[m, t], sq_recv.at[m, frm], (frm, sec)).wait_recv()
        return sq_in[m, frm]

    def next_copy(m):
        return remote(done.at[m], xs.at[m], z_send.at[m], z_recv.at[m], (me, sec + 1))

    def back_copy(m):
        return remote(done.at[m], back, b_send.at[m], b_recv.at[0], (me, m))

    def home_copy(t):
        to = lax.rem(me + t, owners)
        piece = back.at[pl.ds(to * cards, cards)]
        return remote(piece, home.at[me], r_send.at[t], r_recv.at[me], (to, sec))

    def enter(m):
        @pl.when(sec + m > 0)
        def _():
            remote(xs.at[m], xs.at[m], z_send.at[m], z_recv.at[m], (me, 0)).wait_recv()

        u = xs[m].astype(jnp.float32)
        h = (u * gain_ref[...]).astype(jnp.bfloat16)
        sq = jnp.broadcast_to(jnp.sum(u * u, axis=1, keepdims=True), (rows, LANES))
        sq_out[m] = jnp.transpose(sq)[:8]
        for t in range(1, owners):
            sq_copy(m, t).start()
        share(m, lambda k: jnp.dot(h, weight[:, cols(k)], preferred_element_type=jnp.float32))

    def leave(m):
        y = collect(m)
        sq = sq_out[m]
        for t in range(1, owners):
            sq = sq + sq_wait(m, t)
        scale = lax.rsqrt(sq / width + 1e-05)
        y = y * jnp.transpose(scale)[:, :1]
        u = xs[m].astype(jnp.float32)
        done[m] = (u + y / (1.0 + jnp.exp(-y))).astype(jnp.bfloat16)

        @pl.when(sec < last)
        def _():
            next_copy(m).start()

        @pl.when((sec == last) & (m < last))
        def _():
            back_copy(m).start()

    def each(m, carry):
        @pl.when(m < sections)
        def _():
            enter(m)

        @pl.when(m > 0)
        def _():
            leave(m - 1)

        @pl.when(m < sections)
        def _():
            across(m)

        return carry

    lax.fori_loop(0, sections + 1, each, 0)

    @pl.when(sec == last)
    def _():
        back[...] = done[last]

    @pl.when(sec < last)
    def _():
        remote(back, back, b_send.at[0], b_recv.at[0], (me, last)).wait_recv()

    for t in range(1, owners):
        home_copy(t).start()
    out_ref[:, cols(me)] = back[pl.ds(me * cards, cards)]
    for t in range(1, owners):
        frm = lax.rem(me + owners - t, owners)
        remote(home.at[frm], home.at[frm], r_send.at[t], r_recv.at[frm], (frm, sec)).wait_recv()
        out_ref[:, cols(frm)] = home[frm]
        home_copy(t).wait_send()

    reduced_sends(sections)

    @pl.when(sec > 0)
    def _():
        entry_copy().wait_send()

    def finish(m, carry):
        reduced_sends(m)
        for t in range(1, owners):
            sq_copy(m, t).wait_send()

        @pl.when(sec < last)
        def _():
            next_copy(m).wait_send()

        @pl.when((sec == last) & (m < last))
        def _():
            back_copy(m).wait_send()

        return carry

    lax.fori_loop(0, sections, finish, 0)


def kernel_body(owners, sections, txn_feats, txn_seg, seg_row, send_counts, gains, tower_w):
    width = txn_feats.shape[1]
    fb = width // owners
    cards = CARD_DEV
    rows = owners * cards
    chips = owners // 2
    bf = jnp.bfloat16
    hbm = pl.BlockSpec(memory_space=pltpu.HBM)
    dma = pltpu.SemaphoreType.DMA
    stages = sections + 1
    return pl.pallas_call(
        functools.partial(tower_kernel, owners, sections, cards),
        out_shape=jax.ShapeDtypeStruct((cards, width), bf),
        in_specs=[hbm] * 6,
        out_specs=pl.BlockSpec(memory_space=pltpu.VMEM),
        scratch_shapes=[
            pltpu.VMEM(txn_seg.shape, jnp.int32),
            pltpu.SMEM(seg_row.shape, jnp.int32),
            pltpu.SMEM(send_counts.shape, jnp.int32),
            pltpu.VMEM((1, fb), jnp.float32),
            pltpu.VMEM(txn_feats.shape, bf),
            pltpu.VMEM((fb, width), bf),
            pltpu.VMEM((stages, chips, rows, fb), bf),
            pltpu.VMEM((stages, chips, rows, fb), bf),
            pltpu.VMEM((chips, rows, fb), jnp.float32),
            pltpu.VMEM((rows, fb), jnp.float32),
            pltpu.VMEM((stages, chips, rows, fb), bf),
            pltpu.VMEM((stages, chips, rows, fb), bf),
            pltpu.VMEM((sections, 8, rows), jnp.float32),
            pltpu.VMEM((sections, owners, 8, rows), jnp.float32),
            pltpu.VMEM((rows, fb), bf),
            pltpu.VMEM((sections, rows, fb), bf),
            pltpu.VMEM((sections, rows, fb), bf),
            pltpu.VMEM((rows, fb), bf),
            pltpu.VMEM((owners, cards, fb), bf),
            dma((6,)),
            dma((stages, chips)),
            dma((stages, chips)),
            dma((stages, chips)),
            dma((stages, chips)),
            dma((sections, owners)),
            dma((sections, owners)),
            dma((1,)),
            dma((sections,)),
            dma((sections,)),
            dma((sections,)),
            dma((1,)),
            dma((owners,)),
            dma((owners,)),
        ],
        compiler_params=pltpu.CompilerParams(
            collective_id=0, has_side_effects=True, vmem_limit_bytes=64 * 1024 * 1024
        ),
    )(txn_seg, seg_row, send_counts, gains, txn_feats, tower_w)


def solution(mesh):
    in_specs = (
        P(("ingest", "section"), None),
        P(("ingest", "section"), None),
        P(("ingest", "section"), None),
        P(("ingest", "section"), None),
        P("section", None),
        P("section", "ingest", None),
    )
    out_specs = P(("ingest", "section"), None)
    owners, sections = mesh.shape["ingest"], mesh.shape["section"]

    def body(txn_feats, txn_seg, seg_row, send_counts, gains, tower_w):
        args = (txn_feats, txn_seg, seg_row, send_counts, gains, tower_w)
        if owners % 2 == 0 and owners * CARD_DEV % LANES == 0 and txn_feats.shape[1] % (owners * LANES) == 0:
            return kernel_body(owners, sections, *args)
        return plain_body(*args)

    return jax.shard_map(body, mesh=mesh, in_specs=in_specs, out_specs=out_specs, check_vma=False)
```

```python
import functools

import jax
import jax.numpy as jnp
from jax import lax
from jax.experimental import pallas as pl
from jax.experimental.pallas import tpu as pltpu
from jax.sharding import PartitionSpec as P

MESH = pl.DeviceIdType.MESH
CARD_DEV = 16
LANES = 128

def from_behind(x, axis, by):
    count = lax.axis_size(axis)
    pairs = [(i, i + by) for i in range(count) if 0 <= i + by < count]
    return lax.ppermute(x, axis, pairs)


def broadcast(x, axis, root):
    mine = lax.axis_index(axis) == root
    return lax.psum(jnp.where(mine, x, jnp.zeros_like(x)), axis)


def tower_layer(x, gain, weight):
    u = x.astype(jnp.float32)
    mean_sq = jnp.mean(u * u, axis=-1, keepdims=True)
    normed = (u * lax.rsqrt(mean_sq + 1e-05) * gain).astype(jnp.bfloat16)
    y = jnp.dot(normed, weight, preferred_element_type=jnp.float32)
    return (u + jax.nn.silu(y)).astype(jnp.bfloat16)


def plain_body(txn_feats, txn_seg, seg_row, send_counts, gains, tower_w):
    width = txn_feats.shape[1]
    owners = lax.axis_size("ingest")
    sections = lax.axis_size("section")
    slots = seg_row.shape[1]
    cards = CARD_DEV
    weight = lax.all_gather(tower_w[0], "ingest", axis=0, tiled=True)
    gain = gains[0]
    counts = send_counts[0]
    ends = jnp.cumsum(counts)
    seg = txn_seg[0]
    rows = seg_row[0]
    slot_ids = jnp.arange(slots, dtype=jnp.int32)
    txn_owner = jnp.sum((seg[:, None] >= ends[None, :]).astype(jnp.int32), axis=1)
    txn_row = jnp.sum((seg[:, None] == slot_ids[None, :]).astype(jnp.int32) * rows[None, :], axis=1)
    target = txn_owner * cards + txn_row
    place = (jnp.arange(owners * cards, dtype=jnp.int32)[:, None] == target[None, :]).astype(
        jnp.bfloat16
    )
    buffer = jnp.dot(place, txn_feats, preferred_element_type=jnp.float32).astype(jnp.bfloat16)
    buffer = buffer.reshape(owners, cards, width)
    received = lax.all_to_all(buffer, "ingest", split_axis=0, concat_axis=0, tiled=True)
    pooled = jnp.sum(received, axis=0, dtype=jnp.float32).astype(jnp.bfloat16)
    section_pos = lax.axis_index("section")
    total_steps = 2 * sections - 1
    blocks = lax.all_gather(pooled[None], "section", axis=0, tiled=True)

    def advance(step, carry):
        current, finished, waiting = carry
        incoming = from_behind(current, "section", 1)
        fresh = lax.dynamic_index_in_dim(blocks, jnp.minimum(step, sections - 1), 0, keepdims=False)
        entry = jnp.where(section_pos == 0, fresh, incoming)
        active = (step >= section_pos) & (step < section_pos + sections)
        result = lax.cond(active, lambda v: tower_layer(v, gain, weight), lambda v: v, entry)
        place_at = jnp.clip(step - (sections - 1), 0, sections - 1)
        keep = (section_pos == sections - 1) & (step >= sections - 1)
        before = lax.dynamic_index_in_dim(finished, place_at, 0, keepdims=False)
        finished = lax.dynamic_update_index_in_dim(
            finished, jnp.where(keep, result, before), place_at, 0
        )
        return (result, finished, waiting)

    start_state = (
        jnp.zeros_like(pooled),
        jnp.zeros((sections, cards, width), jnp.bfloat16),
        pooled,
    )
    final_state = lax.fori_loop(0, total_steps, advance, start_state)
    everything = broadcast(final_state[1], "section", sections - 1)
    return lax.dynamic_index_in_dim(everything, section_pos, 0, keepdims=False)


def tower_kernel(
    owners, sections, cards,
    seg_hbm, row_hbm, count_hbm, gain_hbm, feats_hbm, w_hbm, out_ref,
    seg_ref, row_ref, count_ref, gain_ref, feats, weight,
    sib_out, sib_in, own, total_ref, cross_out, cross_in, sq_out, sq_in, pooled, xs, done, back, home,
    local_sem, sib_send, sib_recv, cross_send, cross_recv, sq_send, sq_recv,
    x_send, z_send, z_recv, b_send, b_recv, r_send, r_recv,
):
    me = lax.axis_index("ingest")
    sec = lax.axis_index("section")
    last = sections - 1
    width = feats.shape[1]
    fb = width // owners
    rows = owners * cards
    slots = row_ref.shape[1]
    core = lax.rem(me, 2)
    sibling = me + 1 - 2 * core
    chip = me // 2
    chips = owners // 2

    def remote(src, dst, send, recv, to):
        return pltpu.make_async_remote_copy(
            src_ref=src, dst_ref=dst, send_sem=send, recv_sem=recv, device_id=to, device_id_type=MESH
        )

    def cols(k):
        return pl.ds(pl.multiple_of(k * fb, LANES), fb)

    loads = [
        pltpu.make_async_copy(source, to, local_sem.at[n])
        for n, (source, to) in enumerate((
            (seg_hbm, seg_ref), (row_hbm, row_ref), (count_hbm, count_ref),
            (feats_hbm, feats), (gain_hbm.at[:, cols(me)], gain_ref), (w_hbm.at[0], weight),
        ))
    ]
    for load in loads:
        load.start()

    barrier = pltpu.get_barrier_semaphore()

    for t in range(1, owners):
        pl.semaphore_signal(
            barrier, inc=1, device_id=(lax.rem(me + t, owners), sec), device_id_type=MESH
        )
    for t in range(1, sections):
        pl.semaphore_signal(
            barrier, inc=1, device_id=(me, lax.rem(sec + t, sections)), device_id_type=MESH
        )
    for load in loads[:3]:
        load.wait()

    seg = seg_ref[...]
    owner = jnp.zeros_like(seg)
    end = count_ref[0, 0]
    for j in range(owners):
        if j > 0:
            end = end + count_ref[0, j]
        owner = owner + (seg >= end).astype(jnp.int32)
    row = jnp.zeros_like(seg)
    for g in range(slots):
        row = jnp.where(seg == g, row_ref[0, g], row)
    target = owner * cards + row
    ids = lax.broadcasted_iota(jnp.int32, (rows, seg.shape[1]), 0)
    place = jnp.where(ids == target, 1.0, 0.0).astype(jnp.bfloat16)
    loads[3].wait()

    def ahead(d):
        return lax.rem(chip + d, chips)

    def behind(d):
        return lax.rem(chip + chips - d, chips)

    def sib_copy(q, d):
        c = ahead(d)
        return remote(sib_out.at[q, c], sib_in.at[q, c], sib_send.at[q, d], sib_recv.at[q, c], (sibling, sec))

    def cross_copy(q, d):
        return remote(
            cross_out.at[q, d], cross_in.at[q, chip], cross_send.at[q, d], cross_recv.at[q, chip],
            (ahead(d) * 2 + core, sec),
        )

    def cross_wait(q, d):
        c = behind(d)
        remote(
            cross_out.at[q, d], cross_in.at[q, c], cross_send.at[q, d], cross_recv.at[q, c], (c * 2 + core, sec)
        ).wait_recv()

    order = list(range(1, chips)) + [0]

    def share(q, product):
        for d in order:
            c = ahead(d)
            sib_out[q, c] = product(c * 2 + 1 - core).astype(jnp.bfloat16)
            sib_copy(q, d).start()

    def keep(product):
        for d in order:
            own[d] = product(ahead(d) * 2 + core)

    def across(q):
        for d in order[:-1]:
            sib_copy(q, d).wait_recv()
            cross_out[q, d] = (own[d] + sib_in[q, ahead(d)].astype(jnp.float32)).astype(jnp.bfloat16)
            cross_copy(q, d).start()
        sib_copy(q, 0).wait_recv()
        total_ref[...] = own[0] + sib_in[q, chip].astype(jnp.float32)

    def collect(q):
        total = total_ref[...]
        for d in order[:-1]:
            cross_wait(q, d)
            total = total + cross_in[q, behind(d)].astype(jnp.float32)
        return total

    def reduced_sends(q):
        for d in order:
            sib_copy(q, d).wait_send()
        for d in order[:-1]:
            cross_copy(q, d).wait_send()

    def pool(k):
        return jnp.dot(place, feats[:, cols(k)], preferred_element_type=jnp.float32)

    keep(pool)
    pl.semaphore_wait(barrier, owners + sections - 2)
    share(sections, pool)
    across(sections)
    x0 = collect(sections).astype(jnp.bfloat16)

    def entry_copy():
        return remote(pooled, xs.at[sec], x_send.at[0], z_recv.at[sec], (me, 0))

    @pl.when(sec == 0)
    def _():
        xs[0] = x0

    @pl.when(sec > 0)
    def _():
        pooled[...] = x0
        entry_copy().start()

    loads[4].wait()
    loads[5].wait()

    def sq_copy(m, t):
        to = lax.rem(me + t, owners)
        return remote(sq_out.at[m], sq_in.at[m, me], sq_send.at[m, t], sq_recv.at[m, me], (to, sec))

    def sq_wait(m, t):
        frm = lax.rem(me + owners - t, owners)
        remote(sq_out.at[m], sq_in.at[m, frm], sq_send.at[m, t], sq_recv.at[m, frm], (frm, sec)).wait_recv()
        return sq_in[m, frm]

    def next_copy(m):
        return remote(done.at[m], xs.at[m], z_send.at[m], z_recv.at[m], (me, sec + 1))

    def back_copy(m):
        return remote(done.at[m], back, b_send.at[m], b_recv.at[0], (me, m))

    def home_copy(t):
        to = lax.rem(me + t, owners)
        piece = back.at[pl.ds(to * cards, cards)]
        return remote(piece, home.at[me], r_send.at[t], r_recv.at[me], (to, sec))

    def enter(m):
        @pl.when(sec + m > 0)
        def _():
            remote(xs.at[m], xs.at[m], z_send.at[m], z_recv.at[m], (me, 0)).wait_recv()

        u = xs[m].astype(jnp.float32)
        h = (u * gain_ref[...]).astype(jnp.bfloat16)

        def layer(k):
            return jnp.dot(h, weight[:, cols(k)], preferred_element_type=jnp.float32)

        share(m, layer)
        sq = jnp.broadcast_to(jnp.sum(u * u, axis=1, keepdims=True), (rows, LANES))
        sq_out[m] = jnp.transpose(sq)[:8]
        for t in range(1, owners):
            sq_copy(m, t).start()
        keep(layer)

    def leave(m):
        y = collect(m)
        sq = sq_out[m]
        for t in range(1, owners):
            sq = sq + sq_wait(m, t)
        scale = lax.rsqrt(sq / width + 1e-05)
        y = y * jnp.transpose(scale)[:, :1]
        u = xs[m].astype(jnp.float32)
        done[m] = (u + y / (1.0 + jnp.exp(-y))).astype(jnp.bfloat16)

        @pl.when(sec < last)
        def _():
            next_copy(m).start()

        @pl.when((sec == last) & (m < last))
        def _():
            back_copy(m).start()

    def each(m, carry):
        @pl.when(m < sections)
        def _():
            enter(m)

        @pl.when(m > 0)
        def _():
            leave(m - 1)

        @pl.when(m < sections)
        def _():
            across(m)

        return carry

    lax.fori_loop(0, sections + 1, each, 0)

    @pl.when(sec == last)
    def _():
        back[...] = done[last]

    @pl.when(sec < last)
    def _():
        remote(back, back, b_send.at[0], b_recv.at[0], (me, last)).wait_recv()

    for t in range(1, owners):
        home_copy(t).start()
    out_ref[:, cols(me)] = back[pl.ds(me * cards, cards)]
    for t in range(1, owners):
        frm = lax.rem(me + owners - t, owners)
        remote(home.at[frm], home.at[frm], r_send.at[t], r_recv.at[frm], (frm, sec)).wait_recv()
        out_ref[:, cols(frm)] = home[frm]
        home_copy(t).wait_send()

    reduced_sends(sections)

    @pl.when(sec > 0)
    def _():
        entry_copy().wait_send()

    def finish(m, carry):
        reduced_sends(m)
        for t in range(1, owners):
            sq_copy(m, t).wait_send()

        @pl.when(sec < last)
        def _():
            next_copy(m).wait_send()

        @pl.when((sec == last) & (m < last))
        def _():
            back_copy(m).wait_send()

        return carry

    lax.fori_loop(0, sections, finish, 0)


def kernel_body(owners, sections, txn_feats, txn_seg, seg_row, send_counts, gains, tower_w):
    width = txn_feats.shape[1]
    fb = width // owners
    cards = CARD_DEV
    rows = owners * cards
    chips = owners // 2
    bf = jnp.bfloat16
    hbm = pl.BlockSpec(memory_space=pltpu.HBM)
    dma = pltpu.SemaphoreType.DMA
    stages = sections + 1
    return pl.pallas_call(
        functools.partial(tower_kernel, owners, sections, cards),
        out_shape=jax.ShapeDtypeStruct((cards, width), bf),
        in_specs=[hbm] * 6,
        out_specs=pl.BlockSpec(memory_space=pltpu.VMEM),
        scratch_shapes=[
            pltpu.VMEM(txn_seg.shape, jnp.int32),
            pltpu.SMEM(seg_row.shape, jnp.int32),
            pltpu.SMEM(send_counts.shape, jnp.int32),
            pltpu.VMEM((1, fb), jnp.float32),
            pltpu.VMEM(txn_feats.shape, bf),
            pltpu.VMEM((fb, width), bf),
            pltpu.VMEM((stages, chips, rows, fb), bf),
            pltpu.VMEM((stages, chips, rows, fb), bf),
            pltpu.VMEM((chips, rows, fb), jnp.float32),
            pltpu.VMEM((rows, fb), jnp.float32),
            pltpu.VMEM((stages, chips, rows, fb), bf),
            pltpu.VMEM((stages, chips, rows, fb), bf),
            pltpu.VMEM((sections, 8, rows), jnp.float32),
            pltpu.VMEM((sections, owners, 8, rows), jnp.float32),
            pltpu.VMEM((rows, fb), bf),
            pltpu.VMEM((sections, rows, fb), bf),
            pltpu.VMEM((sections, rows, fb), bf),
            pltpu.VMEM((rows, fb), bf),
            pltpu.VMEM((owners, cards, fb), bf),
            dma((6,)),
            dma((stages, chips)),
            dma((stages, chips)),
            dma((stages, chips)),
            dma((stages, chips)),
            dma((sections, owners)),
            dma((sections, owners)),
            dma((1,)),
            dma((sections,)),
            dma((sections,)),
            dma((sections,)),
            dma((1,)),
            dma((owners,)),
            dma((owners,)),
        ],
        compiler_params=pltpu.CompilerParams(
            collective_id=0, has_side_effects=True, vmem_limit_bytes=64 * 1024 * 1024
        ),
    )(txn_seg, seg_row, send_counts, gains, txn_feats, tower_w)


def solution(mesh):
    in_specs = (
        P(("ingest", "section"), None),
        P(("ingest", "section"), None),
        P(("ingest", "section"), None),
        P(("ingest", "section"), None),
        P("section", None),
        P("section", "ingest", None),
    )
    out_specs = P(("ingest", "section"), None)
    owners, sections = mesh.shape["ingest"], mesh.shape["section"]

    def body(txn_feats, txn_seg, seg_row, send_counts, gains, tower_w):
        args = (txn_feats, txn_seg, seg_row, send_counts, gains, tower_w)
        if owners % 2 == 0 and owners * CARD_DEV % LANES == 0 and txn_feats.shape[1] % (owners * LANES) == 0:
            return kernel_body(owners, sections, *args)
        return plain_body(*args)

    return jax.shard_map(body, mesh=mesh, in_specs=in_specs, out_specs=out_specs, check_vma=False)
```
